32 devices in a mesh: dp: 8 (over y, x, core), mp: 4 (over z).
Axes of the slice: x: 2, y: 2, z: 4, core: 2. Of those that a mesh axis runs over, the one named last changes fastest.
Arguments:
- prefix_in: bfloat16 [8, 512, 2048], P('dp', 'mp'), may hold values from -6 to 6
- action_in: bfloat16 [8, 50, 1024], P('dp'), may hold values from -6 to 6
- prefix_len: int32 [8], P('dp'), may hold values from 448 to 512, as said below
- action_count: int32 [8], P('dp'), may hold values from 25 to 50, as said below
- loss_weight: int32 [8], P('dp'), may hold values from 1 to 4
- prefix_gains: bfloat16 [2048, 2], P(('dp', 'mp')), may hold values from 0.099609375 to 1.8984375
- action_gains: bfloat16 [1024, 2], P(('dp', 'mp')), may hold values from 0.099609375 to 1.8984375
- prefix_qkv: bfloat16 [2048, 2560], P(('dp', 'mp')), may hold values from -0.125 to 0.125
- prefix_out_proj: bfloat16 [2048, 2048], P(('dp', 'mp')), may hold values from -0.75 to 0.75
- action_qkv: bfloat16 [1024, 2560], P(('dp', 'mp')), may hold values from -0.1875 to 0.1875
- action_out_proj: bfloat16 [2048, 1024], P(('dp', 'mp')), may hold values from -0.75 to 0.75
- prefix_gate_up: bfloat16 [2, 2048, 16384], P(None, 'dp', 'mp'), may hold values from -0.125 to 0.125
- prefix_down: bfloat16 [16384, 2048], P('mp', 'dp'), may hold values from -0.09375 to 0.09375
- action_gate_up: bfloat16 [2, 1024, 4096], P(None, 'dp', 'mp'), may hold values from -0.1875 to 0.1875
- action_down: bfloat16 [4096, 1024], P('mp', 'dp'), may hold values from -0.1875 to 0.1875
- prefix_cot: bfloat16 [8, 512, 2048], P('dp', 'mp'), may hold values from -6 to 6
- action_cot: bfloat16 [8, 50, 1024], P('dp'), may hold values from -6 to 6
Outputs:
- prefix_out: bfloat16 [8, 512, 2048], P('dp', 'mp')
- action_out: bfloat16 [8, 50, 1024], P('dp')
- prefix_in_grad: float32 [8, 512, 2048], P('dp', 'mp')
- action_in_grad: float32 [8, 50, 1024], P('dp')
- prefix_gains_grad: float32 [2048, 2], P(('dp', 'mp'))
- action_gains_grad: float32 [1024, 2], P(('dp', 'mp'))
- prefix_qkv_grad: float32 [2048, 2560], P(('dp', 'mp'))
- prefix_out_proj_grad: float32 [2048, 2048], P(('dp', 'mp'))
- action_qkv_grad: float32 [1024, 2560], P(('dp', 'mp'))
- action_out_proj_grad: float32 [2048, 1024], P(('dp', 'mp'))
- prefix_gate_up_grad: float32 [2, 2048, 16384], P(None, 'dp', 'mp')
- prefix_down_grad: float32 [16384, 2048], P('mp', 'dp')
- action_gate_up_grad: float32 [2, 1024, 4096], P(None, 'dp', 'mp')
- action_down_grad: float32 [4096, 1024], P('mp', 'dp')
The draws below stay inside these ranges and needn't reach their ends.
Inputs may be any that keep to these rules, and one draw needn't show every extreme that they name: `prefix_len`: some item counts all 512 positions in every draw. `action_count`: some item counts all 50 action tokens in every draw.
All inputs are finite; a program needn't handle non-finite values.
Results may differ from the reference program's by a relative error of at most 0.02.
Values may be sent and summed in bfloat16 or wider, within the bound.
No kernel may reach another device: no remote copies, remote signals or barrier semaphores. Data moves between devices by JAX's collectives and lax.ppermute only.
A program may use at most 256 MiB of HBM per device.

```python
import math
import jax
import jax.numpy as jnp
from jax import lax

D = 2048
FF = 16384
DA = 1024
FFA = 4096
HEADS = 8
HD = 256
ACT = 50
PSLAB = 128
PREFIX = 512
ITEMS = 8


def forced_top(key, least_value, top_value):
    base = jax.random.randint(key, (ITEMS,), least_value, top_value + 1)
    pick = jax.random.randint(jax.random.fold_in(key, 11), (), 0, ITEMS)
    return jnp.where(jnp.arange(ITEMS) == pick, top_value, base).astype(jnp.int32)


def draw_prefix_len(key, part):
    return forced_top(key, PREFIX - PSLAB // 2, PREFIX)


def draw_action_count(key, part):
    return forced_top(key, ACT // 2, ACT)


def with_ends(values, key, smallest, high):
    longest = values.shape.index(max(values.shape))
    spots = []
    for shift in (0, 1):
        where = [jax.random.randint(jax.random.fold_in(key, axis), (), 0, length) for axis, length in enumerate(values.shape)]
        where[longest] = (where[longest] + shift) % values.shape[longest]
        spots.append(tuple(where))
    return values.at[spots[0]].set(smallest).at[spots[1]].set(high)


def shard_levels(stream_key, extent, cuts, smallest, largest):
    level = 1.0
    for position, shards_of in cuts:
        heights = jax.random.uniform(jax.random.fold_in(jax.random.fold_in(stream_key, 6), position), (shards_of,), jnp.float32, smallest / len(cuts), largest / len(cuts))
        level = level * jnp.repeat(jnp.exp(heights), extent[position] // shards_of).reshape((-1,) + (1,) * (len(extent) - 1 - position))
    return level


def noise(stream_key, shape, spread, most, shards=(), held_as=jnp.bfloat16):
    result = jax.random.normal(stream_key, shape, jnp.float32) * spread
    if len(shards) > 0:
        result = shard_levels(stream_key, shape, shards, -0.22, 0.18) * result
    return jnp.clip(result, min=-most, max=most).astype(held_as)


def setup_inputs(seed: int = 0) -> dict:
    key_list = jax.random.split(jax.random.key(seed), 18)
    prefix_in = noise(key_list[0], (ITEMS, PREFIX, D), 1.0, 6.0, ((0, 8), (1, 4)))
    action_in = noise(key_list[1], (ITEMS, ACT, DA), 1.0, 6.0, ((0, 8),))
    prefix_len = draw_prefix_len(jax.random.fold_in(key_list[17], 71), 0)
    action_count = draw_action_count(jax.random.fold_in(key_list[17], 71), 0)
    loss_weight = with_ends(jax.random.randint(key_list[4], (ITEMS,), 1, 5), jax.random.fold_in(key_list[4], 1), 1, 4).astype(jnp.int32)
    prefix_gains = jnp.clip(1.0 + 0.18 * jax.random.normal(key_list[5], (D, 2), jnp.float32), 0.099609375, 1.8984375).astype(jnp.bfloat16)
    action_gains = jnp.clip(1.0 + 0.18 * jax.random.normal(key_list[6], (DA, 2), jnp.float32), 0.099609375, 1.8984375).astype(jnp.bfloat16)
    prefix_qkv = noise(key_list[7], (D, HEADS * HD + 2 * HD), D ** -0.5, 0.125, ((0, 32),))
    prefix_out_proj = noise(key_list[8], (HEADS * HD, D), (HEADS * HD // 32) ** -0.5, 0.75, ((0, 32),))
    action_qkv = noise(key_list[9], (DA, HEADS * HD + 2 * HD), DA ** -0.5, 0.1875, ((0, 32),))
    action_out_proj = noise(key_list[10], (HEADS * HD, DA), (HEADS * HD // 32) ** -0.5, 0.75, ((0, 32),))
    prefix_gate_up = noise(key_list[11], (2, D, FF), D ** -0.5, 0.125, ((1, 8), (2, 4)))
    prefix_down = noise(key_list[12], (FF, D), (FF // 4) ** -0.5, 0.09375, ((0, 4), (1, 8)))
    action_gate_up = noise(key_list[13], (2, DA, FFA), DA ** -0.5, 0.1875, ((1, 8), (2, 4)))
    action_down = noise(key_list[14], (FFA, DA), (FFA // 4) ** -0.5, 0.1875, ((0, 4), (1, 8)))
    prefix_cot = noise(key_list[15], (ITEMS, PREFIX, D), 1.0, 6.0, ((0, 8), (1, 4)))
    action_cot = noise(key_list[16], (ITEMS, ACT, DA), 1.0, 6.0, ((0, 8),))
    return dict(prefix_in=prefix_in, action_in=action_in, prefix_len=prefix_len, action_count=action_count, loss_weight=loss_weight, prefix_gains=prefix_gains, action_gains=action_gains, prefix_qkv=prefix_qkv, prefix_out_proj=prefix_out_proj, action_qkv=action_qkv, action_out_proj=action_out_proj, prefix_gate_up=prefix_gate_up, prefix_down=prefix_down, action_gate_up=action_gate_up, action_down=action_down, prefix_cot=prefix_cot, action_cot=action_cot)


@jax.custom_vjp
def low(v):
    return lax.optimization_barrier(v.astype(jnp.bfloat16)).astype(jnp.float32)

@jax.custom_vjp
def low_back(v):
    return v

def low_keep(v):
    return (low(v), None)

def low_pass(kept, grad):
    return (grad,)

def back_keep(v):
    return (v, None)

def back_low(kept, grad):
    return (low(grad),)
low.defvjp(low_keep, low_pass)
low_back.defvjp(back_keep, back_low)
EPS = 1e-06

def product(left, right):
    return jnp.matmul(left, right, precision=lax.Precision.HIGHEST)

def rms_norm(values, gain):
    scale = lax.rsqrt(lax.optimization_barrier(jnp.mean(values * values, axis=-1, keepdims=True)) + EPS)
    return values * scale * gain

def attend_item(query, keys, keep):
    heads = query.reshape(query.shape[0], HEADS, HD)
    scores = jnp.einsum('thd,ud->htu', heads, keys[:, :HD], precision=lax.Precision.HIGHEST)
    scores = low_back(scores * (1.0 / math.sqrt(HD)))
    scores = jnp.where(keep[None, None, :], scores, -1e+30)
    probs = jax.nn.softmax(scores, axis=-1)
    mixed = jnp.einsum('htu,ud->thd', low(probs), keys[:, HD:], precision=lax.Precision.HIGHEST)
    return mixed.reshape(query.shape[0], HEADS * HD)

def feed_forward(mid, gain, gate_up, down):
    normed_mid = low(rms_norm(mid, gain))
    gate = low_back(product(normed_mid, gate_up[0]))
    up_part = low_back(product(normed_mid, gate_up[1]))
    hidden = low(jax.nn.gelu(gate, approximate=True) * up_part)
    return low_back(product(hidden, down))

def block(prefix_in, action_in, prefix_gains, action_gains, prefix_qkv, prefix_out_proj, action_qkv, action_out_proj, prefix_gate_up, prefix_down, action_gate_up, action_down, keep_prefix, keep_action):
    width_q = HEADS * HD
    h_prefix = low(rms_norm(prefix_in, prefix_gains[:, 0]))
    h_action = low(rms_norm(action_in, action_gains[:, 0]))
    qkv_prefix = low_back(product(h_prefix, prefix_qkv))
    qkv_action = low_back(product(h_action, action_qkv))
    query_prefix = low(qkv_prefix[..., :width_q])
    kv_prefix = low(qkv_prefix[..., width_q:])
    query_action = low(qkv_action[..., :width_q])
    kv_action = low(qkv_action[..., width_q:])

    def per_item(pieces):
        q_pre, q_act, k_pre, k_act, m_pre, m_act = pieces
        out_pre = attend_item(q_pre, k_pre, m_pre)
        joined = jnp.concatenate([k_pre, k_act], axis=0)
        out_act = attend_item(q_act, joined, jnp.concatenate([m_pre, m_act], axis=0))
        return (out_pre, out_act)
    mixed_prefix, mixed_action = lax.map(jax.checkpoint(per_item), (query_prefix, query_action, kv_prefix, kv_action, keep_prefix, keep_action))
    mixed_prefix = low(low_back(mixed_prefix))
    mixed_action = low(low_back(mixed_action))
    mid_prefix = prefix_in + low_back(product(mixed_prefix, prefix_out_proj))
    mid_action = action_in + low_back(product(mixed_action, action_out_proj))
    out_prefix = mid_prefix + feed_forward(mid_prefix, prefix_gains[:, 1], prefix_gate_up, prefix_down)
    out_action = mid_action + feed_forward(mid_action, action_gains[:, 1], action_gate_up, action_down)
    return (out_prefix, out_action)

def reference(prefix_in, action_in, prefix_len, action_count, loss_weight, prefix_gains, action_gains, prefix_qkv, prefix_out_proj, action_qkv, action_out_proj, prefix_gate_up, prefix_down, action_gate_up, action_down, prefix_cot, action_cot):
    keep_prefix = jnp.arange(PREFIX, dtype=jnp.int32)[None, :] < prefix_len[:, None]
    keep_action = jnp.arange(ACT, dtype=jnp.int32)[None, :] < action_count[:, None]
    floats = [v.astype(jnp.float32) for v in (prefix_in, action_in, prefix_gains, action_gains, prefix_qkv, prefix_out_proj, action_qkv, action_out_proj, prefix_gate_up, prefix_down, action_gate_up, action_down)]

    def forward(*values):
        return block(*values, keep_prefix, keep_action)
    (out_prefix, out_action), pull = jax.vjp(forward, *floats)
    weight = loss_weight.astype(jnp.float32)
    grad_prefix = prefix_cot.astype(jnp.float32) * (weight[:, None] * keep_prefix.astype(jnp.float32))[:, :, None]
    grad_action = action_cot.astype(jnp.float32) * (weight[:, None] * keep_action.astype(jnp.float32))[:, :, None]
    grads = pull((grad_prefix, grad_action))
    return (out_prefix.astype(jnp.bfloat16), out_action.astype(jnp.bfloat16), grads[0], grads[1], grads[2], grads[3], grads[4], grads[5], grads[6], grads[7], grads[8], grads[9], grads[10], grads[11])
```

```python
import math

import jax
import jax.numpy as jnp
from jax import lax
from jax.sharding import PartitionSpec as P

HEADS = 8
HD = 256
WIDTH_Q = HEADS * HD
INNER = 4
BF = jnp.bfloat16
F32 = jnp.float32

EPS = 1e-06


def dot(left, right, contract):
    return lax.dot_general(left, right, (contract, ((), ())), preferred_element_type=F32)


def mm(left, right):
    return dot(left, right, ((1,), (0,)))


def mm_nt(left, right):
    return dot(left, right, ((1,), (1,)))


def mm_tn(left, right):
    return dot(left, right, ((0,), (0,)))


def normed(values, gain):
    scale = lax.rsqrt(jnp.mean(values * values, axis=-1, keepdims=True) + EPS)
    return values * scale * gain


def geglu(gate, up_part):
    return jax.nn.gelu(gate, approximate=True) * up_part


def swap(value, mask):
    size = lax.axis_size("dp")
    return lax.ppermute(value, "dp", [(i, i ^ mask) for i in range(size)])


def shift(value):
    size = lax.axis_size("mp")
    return lax.ppermute(value, "mp", [(i, (i + 1) % size) for i in range(size)])


def ring_gather(value):
    blocks = [value]
    for _ in range(lax.axis_size("mp") - 1):
        blocks.append(shift(blocks[-1]))
    return blocks


def ring_scatter(blocks):
    total = blocks[1] if len(blocks) > 1 else blocks[0]
    for block in blocks[2:]:
        total = shift(total.astype(BF)).astype(F32) + block
    if len(blocks) > 1:
        total = shift(total.astype(BF)).astype(F32) + blocks[0]
    return total


def block_order(masks):
    order = [0]
    for mask in masks:
        order = order + [j ^ mask for j in order]
    return order


def xor_blocks(value, index, count, axis, order=None):
    size = value.shape[axis] // count
    parts = [lax.slice_in_dim(value, j * size, (j + 1) * size, axis=axis) for j in range(count)]
    bit = 1
    while bit < count:
        on = (index & bit) != 0
        parts = [jnp.where(on, parts[j ^ bit], parts[j]) for j in range(count)]
        bit *= 2
    order = order if order is not None else range(count)
    return jnp.concatenate([parts[j] for j in order], axis=axis)


def unxor_blocks(value, index, count, axis, order):
    size = value.shape[axis] // count
    place = {j: p for p, j in enumerate(order)}
    parts = [
        lax.slice_in_dim(value, place[j] * size, (place[j] + 1) * size, axis=axis)
        for j in range(count)
    ]
    bit = 1
    while bit < count:
        on = (index & bit) != 0
        parts = [jnp.where(on, parts[j ^ bit], parts[j]) for j in range(count)]
        bit *= 2
    return jnp.concatenate(parts, axis=axis)


def dp_gather(value, masks):
    for mask in masks:
        value = jnp.concatenate([value, swap(value, mask)], axis=0)
    return value


def dp_scatter(value, masks):
    for mask in reversed(masks):
        half = value.shape[0] // 2
        value = value[:half] + swap(value[half:].astype(BF), mask).astype(F32)
    return value


def inner_exchange(value):
    size = lax.axis_size("dp")
    groups = [list(range(g, g + INNER)) for g in range(0, size, INNER)]
    return lax.all_to_all(value, "dp", 0, 0, axis_index_groups=groups, tiled=True)


def gather_tokens(rows):
    half = rows.shape[1] // 2
    first = jnp.stack(ring_gather(rows[:, :half]))
    first = jnp.stack([first, swap(first, 2)])
    second = jnp.stack([rows[:, half:], swap(rows[:, half:], 2)])
    second = jnp.stack(ring_gather(second), axis=1)
    out = []
    for part in (first, second):
        part = jnp.stack([part, swap(part, 1)])
        out.append(part.reshape(-1, half))
    return out


def scatter_tokens(first, second, rows):
    shard_count = lax.axis_size("mp")
    half = first.shape[1]
    parts = []
    for part in (first, second):
        part = part.reshape(2, 2, shard_count, rows, half)
        parts.append(part[0] + swap(part[1].astype(BF), 1).astype(F32))
    first = parts[0][0] + swap(parts[0][1].astype(BF), 2).astype(F32)
    first = ring_scatter([first[s] for s in range(shard_count)])
    second = ring_scatter([parts[1][:, s] for s in range(shard_count)])
    second = second[0] + swap(second[1].astype(BF), 2).astype(F32)
    return jnp.concatenate([first, second], axis=-1)


def spread(value, axes):
    size = math.prod(lax.axis_size(a) for a in axes)
    return lax.all_to_all(
        jnp.broadcast_to(value[None], (size,) + value.shape), axes, 0, 0, tiled=True
    )


def sum_mp(value):
    return jnp.sum(spread(value.astype(BF), ("mp",)).astype(F32), axis=0)


def scores_of(query, keys, keep):
    raw = jnp.einsum("thd,ud->htu", query, keys[:, :HD], preferred_element_type=F32)
    return jnp.where(keep[None, None, :], raw * (1.0 / math.sqrt(HD)), -1e30)


def attention(query, keys, keep):
    heads = query.reshape(query.shape[0], -1, HD)
    scores = scores_of(heads, keys, keep)
    top = jnp.max(scores, axis=-1, keepdims=True)
    weights = jnp.exp(scores - top)
    probs = weights / jnp.sum(weights, axis=-1, keepdims=True)
    mixed = jnp.einsum("htu,ud->thd", probs.astype(BF), keys[:, HD:], preferred_element_type=F32)
    return (mixed.reshape(query.shape).astype(BF), probs)


def attention_back(query, keys, probs, grad_mixed):
    heads = query.reshape(query.shape[0], -1, HD)
    heads_grad = grad_mixed.reshape(heads.shape)
    grad_probs = jnp.einsum("thd,ud->htu", heads_grad, keys[:, HD:], preferred_element_type=F32)
    inner = jnp.sum(probs * grad_probs, axis=-1, keepdims=True)
    grad_scores = (probs * (grad_probs - inner)).astype(BF)
    scale = 1.0 / math.sqrt(HD)
    grad_query = (
        jnp.einsum("htu,ud->thd", grad_scores, keys[:, :HD], preferred_element_type=F32) * scale
    )
    grad_key = jnp.einsum("htu,thd->ud", grad_scores, heads, preferred_element_type=F32) * scale
    grad_value = jnp.einsum("htu,thd->ud", probs.astype(BF), heads_grad, preferred_element_type=F32)
    return (grad_query.reshape(query.shape), jnp.concatenate([grad_key, grad_value], axis=-1))


def on_device(
    prefix_in,
    action_in,
    prefix_len,
    action_count,
    loss_weight,
    prefix_gains,
    action_gains,
    prefix_qkv,
    prefix_out_proj,
    action_qkv,
    action_out_proj,
    prefix_gate_up,
    prefix_down,
    action_gate_up,
    action_down,
    prefix_cot,
    action_cot,
):
    dp = lax.axis_index("dp")
    z = lax.axis_index("mp")
    dp_count = lax.axis_size("dp")
    shard_count = lax.axis_size("mp")
    outer = dp_count // INNER
    outer_index = dp // INNER
    slab = prefix_in.shape[1]
    width_p = prefix_in.shape[2]
    width_a = action_in.shape[2]
    action_rows = action_in.shape[1]
    whole_len = slab * shard_count
    query_here = WIDTH_Q // shard_count
    outer_masks = []
    mask = INNER
    while mask < dp_count:
        outer_masks.append(mask)
        mask *= 2
    masks_p = [2] + outer_masks + [1]
    masks_a = outer_masks + [2] + [1]
    order_p = block_order(masks_p)
    order_a = block_order(masks_a)
    everywhere = ("dp", "mp")

    rows_gp = prefix_gains.shape[0]
    rows_ga = action_gains.shape[0]
    gains_own = jnp.concatenate([prefix_gains.T.reshape(-1), action_gains.T.reshape(-1)])
    gains_all = spread(gains_own, everywhere).astype(F32)
    gains_p = gains_all[:, : 2 * rows_gp].reshape(-1, 2, rows_gp)
    gains_a = gains_all[:, 2 * rows_gp :].reshape(-1, 2, rows_ga)
    gain_attn_p = gains_p[:, 0].reshape(-1)
    gain_ffn_p = gains_p[:, 1].reshape(-1)
    gain_attn_a = gains_a[:, 0].reshape(-1)
    gain_ffn_a = gains_a[:, 1].reshape(-1)

    def heads_of(weights):
        rows = weights.shape[0]
        query = weights[:, :WIDTH_Q].reshape(rows, shard_count, query_here).transpose(1, 0, 2)
        both = jnp.broadcast_to(weights[None, :, WIDTH_Q:], (shard_count, rows, 2 * HD))
        own = lax.all_to_all(jnp.concatenate([query, both], axis=-1), "mp", 0, 0, tiled=True)
        return own.reshape(shard_count * rows, query_here + 2 * HD)

    total = dp_count * shard_count
    to_heads = [(j, (j % dp_count) * shard_count + j // dp_count) for j in range(total)]
    from_heads = [(b, a) for a, b in to_heads]
    qkv_p = dp_gather(heads_of(prefix_qkv), masks_p)
    qkv_a = dp_gather(heads_of(action_qkv), masks_a)
    out_own = jnp.concatenate([prefix_out_proj, action_out_proj], axis=1)
    out_own = lax.ppermute(out_own, everywhere, to_heads)
    out_both = unxor_blocks(dp_gather(out_own, masks_a), dp, dp_count, 0, order_a)
    out_p = out_both[:, :width_p]
    out_a = out_both[:, width_p:]

    def hidden_of(weights):
        rows, hidden = weights.shape
        cut = weights.reshape(rows, INNER, hidden // INNER).transpose(1, 0, 2)
        own = inner_exchange(cut).reshape(INNER * rows, hidden // INNER)
        for mask in outer_masks[:-1]:
            own = jnp.concatenate([own, swap(own, mask)], axis=0)
        return (own, swap(own, outer_masks[-1]))

    gate_w = hidden_of(prefix_gate_up[0])
    up_w = hidden_of(prefix_gate_up[1])
    down_w = hidden_of(prefix_down.T)

    def hidden_back(first, second):
        value = first + swap(second.astype(BF), outer_masks[-1]).astype(F32)
        for mask in reversed(outer_masks[:-1]):
            half = value.shape[0] // 2
            value = value[:half] + swap(value[half:].astype(BF), mask).astype(F32)
        rows = value.shape[0] // INNER
        value = inner_exchange(value.astype(BF).reshape(INNER, rows, value.shape[1]))
        return value.transpose(1, 0, 2).reshape(rows, -1).astype(F32)

    def hidden_of_a(weights):
        rows, hidden = weights.shape
        cut = weights.reshape(rows, dp_count, hidden // dp_count).transpose(1, 0, 2)
        own = lax.all_to_all(cut, "dp", 0, 0, tiled=True)
        return own.reshape(dp_count * rows, hidden // dp_count)

    def hidden_back_a(value):
        rows = value.shape[0] // dp_count
        value = value.astype(BF).reshape(dp_count, rows, value.shape[1])
        value = lax.all_to_all(value, "dp", 0, 0, tiled=True)
        return value.transpose(1, 0, 2).reshape(rows, -1).astype(F32)

    gate_wa = hidden_of_a(action_gate_up[0])
    up_wa = hidden_of_a(action_gate_up[1])
    down_wa = hidden_of_a(action_down.T)

    position = jnp.arange(whole_len, dtype=jnp.int32)
    ring_index = (z - position // slab + shard_count) % shard_count
    keep_prefix = ring_index * slab + position % slab < prefix_len[0]
    keep_action = jnp.arange(action_rows, dtype=jnp.int32) < action_count[0]
    keep_joined = jnp.concatenate([keep_prefix, keep_action])
    weight = loss_weight[0].astype(F32)
    keep_own = keep_prefix[:slab]
    grad_out_p = prefix_cot[0].astype(F32) * (weight * keep_own.astype(F32))[:, None]
    grad_out_a = action_cot[0].astype(F32) * (weight * keep_action.astype(F32))[:, None]

    x_p = prefix_in[0]
    x_a = action_in[0]
    input_p = x_p.astype(F32)
    input_a = x_a.astype(F32)
    x_all = jnp.concatenate(ring_gather(xor_blocks(x_p, dp, dp_count, 1, order_p)), axis=0)
    h_attn_p = normed(
        x_all.astype(F32), xor_blocks(gain_attn_p, dp, dp_count, 0, order_p)
    ).astype(BF)
    h_attn_a = normed(
        xor_blocks(input_a, dp, dp_count, 1, order_a),
        xor_blocks(gain_attn_a, dp, dp_count, 0, order_a),
    ).astype(BF)
    all_p = mm(h_attn_p, qkv_p).astype(BF)
    all_a = mm(h_attn_a, qkv_a).astype(BF)
    query_p, kv_p = all_p[:, :query_here], all_p[:, query_here:]
    query_a, kv_a = all_a[:, :query_here], all_a[:, query_here:]
    kv_joined = jnp.concatenate([kv_p, kv_a], axis=0)
    mixed_p, probs_p = attention(query_p, kv_p, keep_prefix)
    mixed_a, probs_a = attention(query_a, kv_joined, keep_joined)
    terms = mm(mixed_p, out_p)
    mid_p = input_p + ring_scatter([terms[s * slab : (s + 1) * slab] for s in range(shard_count)])
    mid_a = input_a + sum_mp(mm(mixed_a, out_a))

    h_ffn_p = normed(mid_p, gain_ffn_p).astype(BF)
    h0, h1 = gather_tokens(xor_blocks(h_ffn_p, outer_index, outer, 1))
    g0, g1 = gather_tokens(xor_blocks(grad_out_p.astype(BF), outer_index, outer, 1))
    gate = mm(h0, gate_w[0]) + mm(h1, gate_w[1])
    up_part = mm(h0, up_w[0]) + mm(h1, up_w[1])
    hidden, pull = jax.vjp(geglu, gate, up_part)
    hidden = hidden.astype(BF)
    d_gate, d_up = pull(mm(g0, down_w[0]) + mm(g1, down_w[1]))
    d_gate = d_gate.astype(BF)
    d_up = d_up.astype(BF)
    dh_terms = [mm_nt(d_gate, gate_w[i]) + mm_nt(d_up, up_w[i]) for i in range(2)]
    dh_p = xor_blocks(scatter_tokens(*dh_terms, slab), outer_index, outer, 1)
    out_terms = [mm_nt(hidden, down_w[i]) for i in range(2)]
    ffn_p = xor_blocks(scatter_tokens(*out_terms, slab), outer_index, outer, 1)
    prefix_out = (mid_p + ffn_p).astype(BF)
    gate_grad_p = hidden_back(mm_tn(h0, d_gate), mm_tn(h1, d_gate))
    up_grad_p = hidden_back(mm_tn(h0, d_up), mm_tn(h1, d_up))
    down_grad_p = hidden_back(mm_tn(g0, hidden), mm_tn(g1, hidden)).T

    h_ffn_a = normed(mid_a, gain_ffn_a).astype(BF)
    ha = spread(h_ffn_a, ("dp",)).reshape(-1, width_a)
    ga = spread(grad_out_a.astype(BF), ("dp",)).reshape(-1, width_a)
    hidden_a, pull_a = jax.vjp(geglu, mm(ha, gate_wa), mm(ha, up_wa))
    hidden_a = hidden_a.astype(BF)
    d_gate_a, d_up_a = pull_a(mm(ga, down_wa))
    d_gate_a = d_gate_a.astype(BF)
    d_up_a = d_up_a.astype(BF)
    terms_a = jnp.stack(
        [mm_nt(hidden_a, down_wa), mm_nt(d_gate_a, gate_wa) + mm_nt(d_up_a, up_wa)]
    )
    terms_a = terms_a.reshape(2, dp_count, action_rows, width_a).transpose(1, 0, 2, 3)
    terms_a = lax.all_to_all(terms_a.astype(BF), "dp", 0, 0, tiled=True)
    sums_a = sum_mp(jnp.sum(terms_a.astype(F32), axis=0))
    action_out = (mid_a + sums_a[0]).astype(BF)
    dh_a = sums_a[1]
    gate_grad_a = hidden_back_a(mm_tn(ha, d_gate_a))
    up_grad_a = hidden_back_a(mm_tn(ha, d_up_a))
    down_grad_a = hidden_back_a(mm_tn(ga, hidden_a)).T

    _, pull_ffn_p = jax.vjp(normed, mid_p, gain_ffn_p)
    from_ffn_p, gain_ffn_grad_p = pull_ffn_p(dh_p)
    d_mid_p = grad_out_p + from_ffn_p
    _, pull_ffn_a = jax.vjp(normed, mid_a, gain_ffn_a)
    from_ffn_a, gain_ffn_grad_a = pull_ffn_a(dh_a)
    d_mid_a = grad_out_a + from_ffn_a

    g_mid_p = jnp.concatenate(ring_gather(d_mid_p.astype(BF)), axis=0)
    g_mid_a = d_mid_a.astype(BF)
    out_grad = jnp.concatenate([mm_tn(mixed_p, g_mid_p), mm_tn(mixed_a, g_mid_a)], axis=1)
    out_grad = dp_scatter(xor_blocks(out_grad, dp, dp_count, 0, order_a), masks_a)
    out_grad = lax.ppermute(out_grad.astype(BF), everywhere, from_heads).astype(F32)
    d_mixed_p = mm_nt(g_mid_p, out_p).astype(BF)
    d_mixed_a = mm_nt(g_mid_a, out_a).astype(BF)
    d_query_p, d_kv_p = attention_back(query_p, kv_p, probs_p, d_mixed_p)
    d_query_a, d_kv_joined = attention_back(query_a, kv_joined, probs_a, d_mixed_a)
    d_kv_p = d_kv_p + d_kv_joined[:whole_len]
    d_all_p = jnp.concatenate([d_query_p, d_kv_p], axis=1).astype(BF)
    d_all_a = jnp.concatenate([d_query_a, d_kv_joined[whole_len:]], axis=1).astype(BF)

    def heads_back(value, masks):
        value = dp_scatter(value, masks).astype(BF)
        rows = value.shape[0] // shard_count
        value = value.reshape(shard_count, rows, value.shape[1])
        value = lax.all_to_all(value, "mp", 0, 0, tiled=True).astype(F32)
        query = value[:, :, :query_here].transpose(1, 0, 2).reshape(rows, WIDTH_Q)
        return jnp.concatenate([query, jnp.sum(value[:, :, query_here:], axis=0)], axis=1)

    qkv_grad_p = heads_back(mm_tn(h_attn_p, d_all_p), masks_p)
    qkv_grad_a = heads_back(mm_tn(h_attn_a, d_all_a), masks_a)
    terms = mm_nt(d_all_p, qkv_p)
    dh_attn_p = ring_scatter([terms[s * slab : (s + 1) * slab] for s in range(shard_count)])
    dh_attn_p = unxor_blocks(dh_attn_p, dp, dp_count, 1, order_p)
    dh_attn_a = unxor_blocks(sum_mp(mm_nt(d_all_a, qkv_a)), dp, dp_count, 1, order_a)
    _, pull_attn_p = jax.vjp(normed, input_p, gain_attn_p)
    from_attn_p, gain_attn_grad_p = pull_attn_p(dh_attn_p)
    _, pull_attn_a = jax.vjp(normed, input_a, gain_attn_a)
    from_attn_a, gain_attn_grad_a = pull_attn_a(dh_attn_a)

    once = (z == 0).astype(F32)
    gains_terms = jnp.concatenate(
        [
            jnp.stack([gain_attn_grad_p, gain_ffn_grad_p]).reshape(2, total, rows_gp),
            jnp.stack([gain_attn_grad_a, gain_ffn_grad_a]).reshape(2, total, rows_ga) * once,
        ],
        axis=2,
    ).transpose(1, 0, 2)
    gains_grad = jnp.sum(lax.all_to_all(gains_terms, everywhere, 0, 0, tiled=True), axis=0)
    return (
        prefix_out[None],
        action_out[None],
        (d_mid_p + from_attn_p)[None],
        (d_mid_a + from_attn_a)[None],
        gains_grad[:, :rows_gp].T,
        gains_grad[:, rows_gp:].T,
        qkv_grad_p,
        out_grad[:, :width_p],
        qkv_grad_a,
        out_grad[:, width_p:],
        jnp.stack([gate_grad_p, up_grad_p]),
        down_grad_p,
        jnp.stack([gate_grad_a, up_grad_a]),
        down_grad_a,
    )


def solution(mesh):
    rows = P(("dp", "mp"), None)
    tokens_p = P("dp", "mp", None)
    tokens_a = P("dp", None, None)
    gate_up = P(None, "dp", "mp")
    down = P("mp", "dp")
    per_item = P("dp")
    in_specs = (
        (tokens_p, tokens_a)
        + (per_item,) * 3
        + (rows,) * 6
        + (gate_up, down, gate_up, down)
        + (tokens_p, tokens_a)
    )
    out_specs = (
        (tokens_p, tokens_a, tokens_p, tokens_a) + (rows,) * 6 + (gate_up, down, gate_up, down)
    )
    return jax.shard_map(
        on_device, mesh=mesh, in_specs=in_specs, out_specs=out_specs, check_vma=False
    )
```

```python
import functools
import math

import jax
import jax.numpy as jnp
from jax import lax
from jax.experimental import pallas as pl
from jax.experimental.pallas import tpu as pltpu
from jax.sharding import PartitionSpec as P

HEADS = 8
HD = 256
WIDTH_Q = HEADS * HD
INNER = 4
BF = jnp.bfloat16
F32 = jnp.float32

EPS = 1e-06


def dot(left, right, contract):
    return lax.dot_general(left, right, (contract, ((), ())), preferred_element_type=F32)


def mm(left, right):
    return dot(left, right, ((1,), (0,)))


def mm_nt(left, right):
    return dot(left, right, ((1,), (1,)))


def mm_tn(left, right):
    return dot(left, right, ((0,), (0,)))


def tie(*values):
    return lax.optimization_barrier(values)


def normed(values, gain):
    scale = lax.rsqrt(jnp.mean(values * values, axis=-1, keepdims=True) + EPS)
    return values * scale * gain


def geglu(gate, up_part):
    return jax.nn.gelu(gate, approximate=True) * up_part


def swap(value, mask):
    size = lax.axis_size("dp")
    return lax.ppermute(value, "dp", [(i, i ^ mask) for i in range(size)])


def bit_of(mask):
    return (lax.axis_index("dp") // mask) % 2


def join(own, other, bit, axis):
    shape = [1] * (own.ndim + 1)
    shape[axis] = 2
    here = (jnp.arange(2, dtype=jnp.int32) == bit).reshape(shape)
    return jnp.where(here, jnp.expand_dims(own, axis), jnp.expand_dims(other, axis))


def dp_gather(value, masks, done=()):
    done = list(done)
    for mask in masks:
        axis = sum(m > mask for m in done)
        value = join(value, swap(value, mask), bit_of(mask), axis)
        done.append(mask)
    return value


def dp_scatter(value, masks, steps=None):
    left = list(masks)
    end = len(left) - steps if steps else 0
    while len(left) > end:
        mask = left.pop()
        axis = sum(m > mask for m in left)
        bit = bit_of(mask)
        other = lax.dynamic_index_in_dim(value, 1 - bit, axis, keepdims=False).astype(BF)
        own = lax.dynamic_index_in_dim(value, bit, axis, keepdims=False)
        value = own.astype(F32) + swap(other, mask).astype(F32)
    return value


def exchange(value, axes="mp"):
    return lax.all_to_all(value, axes, 0, 0, tiled=True)


def spread(value):
    return exchange(jnp.broadcast_to(value[None], (lax.axis_size("mp"),) + value.shape))


def shift(value, steps):
    size = lax.axis_size("mp")
    return lax.ppermute(value, "mp", [(i, (i + steps) % size) for i in range(size)])


def ring(value):
    return [value] + [shift(value, s) for s in range(1, lax.axis_size("mp"))]


def unring(blocks, axis):
    size = blocks[0].shape[axis]
    twice = jnp.concatenate((blocks[:1] + blocks[:0:-1]) * 2, axis=axis)
    count = len(blocks)
    start = (count - lax.axis_index("mp")) % count * size
    return lax.dynamic_slice_in_dim(twice, start, count * size, axis)


def fold(rows_a, width):
    times = width // rows_a.shape[-1]
    n = rows_a.shape[-2] // times
    return jnp.concatenate([rows_a[..., i * n : (i + 1) * n, :] for i in range(times)], axis=-1)


def unfold(rows, width):
    times = rows.shape[-1] // width
    return jnp.concatenate(
        [rows[..., i * width : (i + 1) * width] for i in range(times)], axis=-2
    )


def tokens_of(blocks, slab, width_a):
    prefix = jnp.concatenate([block[:, :slab].reshape(-1, block.shape[2]) for block in blocks])
    action = jnp.concatenate([block[:, slab:].reshape(-1, block.shape[2]) for block in blocks])
    return prefix, unfold(action, width_a)


def sum_cores(prefix, action, slab):
    shard_count = lax.axis_size("mp")
    prefix = prefix.reshape(4, shard_count, slab, -1)
    action = fold(action, prefix.shape[-1]).reshape(4, shard_count, -1, prefix.shape[-1])
    near, far, near_core, far_core = [
        jnp.concatenate([prefix[k], action[k]], axis=1) for k in range(4)
    ]
    far = (far.astype(F32) + swap(far_core, 1).astype(F32)).astype(BF)
    near = (near.astype(F32) + swap(near_core, 1).astype(F32)).astype(BF)
    return near, far


def ffn_kernel(
    places_ref,
    h_ref,
    g_ref,
    *refs,
    pieces_up,
    pieces_down,
):
    up_refs = refs[:pieces_up]
    down_refs = refs[pieces_up : pieces_up + pieces_down]
    act_ref, d_both_ref, dh_ref, gate_up, down, sems = refs[pieces_up + pieces_down :]

    @pl.when(pl.program_id(0) == 0)
    def _():
        copies = []
        rows = gate_up.shape[0] // pieces_up
        for j, ref in enumerate(up_refs):
            place = places_ref[j] if pieces_up > 1 else 0
            target = gate_up.at[pl.ds(pl.multiple_of(place * rows, rows), rows)]
            copies.append(pltpu.make_async_copy(ref, target, sems.at[j]))
        for j, ref in enumerate(down_refs):
            place = places_ref[j] if pieces_down > 1 else 0
            copies.append(pltpu.make_async_copy(ref, down.at[place], sems.at[pieces_up + j]))
        for copy in copies:
            copy.start()
        for copy in copies:
            copy.wait()

    hidden = act_ref.shape[1]
    both = mm(h_ref[...], gate_up[...])
    gate, up_part = both[:, :hidden], both[:, hidden:]
    d_act = jnp.zeros(gate.shape, F32)
    width = down.shape[2]
    for k in range(pieces_down):
        d_act = d_act + mm_nt(g_ref[:, k * width : (k + 1) * width], down[k])
    root = math.sqrt(2.0 / math.pi)
    square = gate * gate
    tanh = jnp.tanh(root * gate * (1.0 + 0.044715 * square))
    plus = 0.5 * (1.0 + tanh)
    gelu = gate * plus
    slope = plus + 0.5 * gate * (1.0 - tanh * tanh) * (root * (1.0 + 3 * 0.044715 * square))
    act_ref[...] = (gelu * up_part).astype(BF)
    d_both_ref[:, :hidden] = (d_act * up_part * slope).astype(BF)
    d_both_ref[:, hidden:] = (d_act * gelu).astype(BF)
    dh_ref[...] = mm_nt(d_both_ref[...], gate_up[...]).astype(BF)


def feed_forward(h, g, places, up_pieces, down_pieces):
    tokens, width = h.shape
    block = min(tokens, 256)
    hidden = down_pieces[0].shape[0]
    count_up, count_down = len(up_pieces), len(down_pieces)

    def rows(columns):
        return pl.BlockSpec((block, columns), lambda i, places: (i, 0))

    return pl.pallas_call(
        functools.partial(ffn_kernel, pieces_up=count_up, pieces_down=count_down),
        grid_spec=pltpu.PrefetchScalarGridSpec(
            num_scalar_prefetch=1,
            grid=(tokens // block,),
            in_specs=[rows(width), rows(width)]
            + [pl.BlockSpec(memory_space=pl.ANY)] * (count_up + count_down),
            out_specs=[rows(hidden), rows(2 * hidden), rows(width)],
            scratch_shapes=[
                pltpu.VMEM((width, 2 * hidden), BF),
                pltpu.VMEM((count_down,) + down_pieces[0].shape, BF),
                pltpu.SemaphoreType.DMA((count_up + count_down,)),
            ],
        ),
        out_shape=[
            jax.ShapeDtypeStruct((tokens, hidden), BF),
            jax.ShapeDtypeStruct((tokens, 2 * hidden), BF),
            jax.ShapeDtypeStruct((tokens, width), BF),
        ],
        compiler_params=pltpu.CompilerParams(vmem_limit_bytes=44 * 2**20),
        name="ffn",
    )(places, h, g, *up_pieces, *down_pieces)


def down_kernel(places_ref, act_ref, *refs):
    down_refs, out_ref = refs[:-1], refs[-1]
    width = out_ref.shape[1] // len(down_refs)
    for j, ref in enumerate(down_refs):
        place = pl.multiple_of(places_ref[j] * width, width)
        out_ref[:, pl.ds(place, width)] = mm(act_ref[...], ref[...]).astype(BF)


def down_product(act, places, down_pieces):
    tokens, hidden = act.shape
    block = min(tokens, 512)
    width = len(down_pieces) * down_pieces[0].shape[1]
    whole = pl.BlockSpec(down_pieces[0].shape, lambda i, places: (0, 0))
    return pl.pallas_call(
        down_kernel,
        grid_spec=pltpu.PrefetchScalarGridSpec(
            num_scalar_prefetch=1,
            grid=(tokens // block,),
            in_specs=[pl.BlockSpec((block, hidden), lambda i, places: (i, 0))]
            + [whole] * len(down_pieces),
            out_specs=pl.BlockSpec((block, width), lambda i, places: (i, 0)),
        ),
        out_shape=jax.ShapeDtypeStruct((tokens, width), BF),
        compiler_params=pltpu.CompilerParams(vmem_limit_bytes=32 * 2**20),
        name="down",
    )(places, act, *down_pieces)


def rows_of_heads(values):
    return jnp.concatenate(
        [values[:, i : i + HD] for i in range(0, values.shape[1], HD)], axis=0
    )


def heads_of_rows(values, heads):
    n = values.shape[0] // heads
    return jnp.concatenate([values[i * n : (i + 1) * n] for i in range(heads)], axis=1)


def on_device(
    prefix_in,
    action_in,
    prefix_len,
    action_count,
    loss_weight,
    prefix_gains,
    action_gains,
    prefix_qkv,
    prefix_out_proj,
    action_qkv,
    action_out_proj,
    prefix_gate_up,
    prefix_down,
    action_gate_up,
    action_down,
    prefix_cot,
    action_cot,
):
    dp = lax.axis_index("dp")
    z = lax.axis_index("mp")
    dp_count = lax.axis_size("dp")
    shard_count = lax.axis_size("mp")
    slab = prefix_in.shape[1]
    width_p = prefix_in.shape[2]
    width_a = action_in.shape[2]
    action_rows = action_in.shape[1]
    whole_len = slab * shard_count
    query_here = WIDTH_Q // shard_count
    heads_here = query_here // HD
    slab_a = -(-action_rows // (16 * shard_count)) * 16
    whole_a = slab_a * shard_count
    outer_masks = []
    mask = INNER
    while mask < dp_count:
        outer_masks.append(mask)
        mask *= 2
    masks_p = [2] + outer_masks + [1]
    masks_a = outer_masks + [2] + [1]
    everywhere = ("dp", "mp")
    cut = width_p * 5 // 8
    total = dp_count * shard_count
    outer = dp_count // INNER
    inner = dp % INNER

    rows_qp = prefix_qkv.shape[0]
    width_kv = query_here + 2 * HD
    own_gain_p = prefix_gains[:, :1].astype(F32)
    own_gain_a = action_gains[:, :1].astype(F32)
    both = jnp.concatenate(
        [prefix_qkv.astype(F32) * own_gain_p, action_qkv.astype(F32) * own_gain_a], axis=0
    ).astype(BF)
    both = jnp.stack(
        [
            jnp.concatenate(
                [both[:, k * query_here : (k + 1) * query_here], both[:, WIDTH_Q:]], axis=1
            )
            for k in range(shard_count)
        ]
    )
    gains_own = jnp.concatenate([prefix_gains[:, 1], action_gains[:, 1]])
    gains_own = jnp.pad(gains_own[None], ((0, 7), (0, width_kv - gains_own.shape[0])))
    both = jnp.concatenate(
        [both, jnp.broadcast_to(gains_own[None], (shard_count,) + gains_own.shape)], axis=1
    )
    both = exchange(both)
    to_heads = [(j, (j % dp_count) * shard_count + j // dp_count) for j in range(total)]
    from_heads = [(b, a) for a, b in to_heads]
    out_own = jnp.concatenate([prefix_out_proj, action_out_proj], axis=1)
    out_own = lax.ppermute(out_own, everywhere, to_heads)
    hidden_p = prefix_down.shape[0] // INNER
    hidden_a = action_down.shape[0] // INNER
    rows_p = prefix_down.shape[1]
    rows_a = action_down.shape[1]

    side, core = bit_of(2), dp % 2

    def half_columns(values, hidden, at):
        gate, up_part = [
            lax.dynamic_slice_in_dim(w, at * 2 * hidden, 2 * hidden, 1) for w in values
        ]
        return jnp.concatenate(
            [gate[:, :hidden], up_part[:, :hidden], gate[:, hidden:], up_part[:, hidden:]], axis=1
        )

    def gate_up_part(at):
        return half_columns(prefix_gate_up, hidden_p, at)

    def down_part(at):
        return lax.dynamic_slice_in_dim(prefix_down, at * 2 * hidden_p, 2 * hidden_p, 0)

    def small_part(at):
        up = half_columns(action_gate_up, hidden_a, at)
        down = lax.dynamic_slice_in_dim(action_down, at * 2 * hidden_a, 2 * hidden_a, 0)
        down = unfold_rows(down.reshape(2, hidden_a, rows_a))
        return jnp.concatenate(
            [up[:, : 2 * hidden_a], down[0], up[:, 2 * hidden_a :], down[1]], axis=1
        )

    def widen(piece):
        pieces = [piece]
        for mask in outer_masks:
            pieces = pieces + [swap(p, mask) for p in pieces]
        return pieces

    def for_cores(piece, axis):
        size = piece.shape[axis] // 2
        own = lax.dynamic_slice_in_dim(piece, core * size, size, axis)
        other = lax.dynamic_slice_in_dim(piece, (1 - core) * size, size, axis)
        return [own, swap(other, 1)]

    keep_prefix = jnp.arange(whole_len, dtype=jnp.int32) < prefix_len[0]
    keep_action = jnp.arange(whole_a, dtype=jnp.int32) < action_count[0]
    weight = loss_weight[0].astype(F32)
    own_p = z * slab + jnp.arange(slab, dtype=jnp.int32) < prefix_len[0]
    own_a = z * slab_a + jnp.arange(slab_a, dtype=jnp.int32) < action_count[0]

    def own_rows_a(values):
        padded = jnp.pad(values[0], ((0, whole_a - action_rows), (0, 0)))
        return padded, lax.dynamic_slice_in_dim(padded, z * slab_a, slab_a, 0)

    _, cot_a = own_rows_a(action_cot)
    grad_out_p = prefix_cot[0].astype(F32) * (weight * own_p.astype(F32))[:, None]
    grad_out_a = cot_a.astype(F32) * (weight * own_a.astype(F32))[:, None]
    x_a, x_own_a = own_rows_a(action_in)
    input_p = prefix_in[0].astype(F32)
    input_a = x_own_a.astype(F32)

    def packed(values_p, values_a):
        return jnp.concatenate([values_p.astype(BF), fold(values_a.astype(BF), width_p)], axis=-2)

    def unpacked(rows):
        return rows[..., :slab, :], unfold(rows[..., slab:, :], width_a)

    down_far, down_near = swap(down_part(1 - side), 2), widen(down_part(side))
    both, out_own, x_all = tie(both, out_own, prefix_in[0])
    x_all = spread(x_all)
    value = both[:, :rows_qp].reshape(-1, width_kv)
    value_a = both[:, rows_qp:].reshape(-1, width_kv)
    out_both = join(out_own, swap(out_own, masks_a[0]), bit_of(masks_a[0]), 0)
    other, down_far, down_near, value_a, out_both = tie(
        swap(value, 2), down_far, down_near, value_a, out_both
    )
    value = join(value, other, bit_of(2), 0)
    done = [2]
    for mask in outer_masks:
        axis = sum(m > mask for m in done)
        value = join(value, swap(value, mask), bit_of(mask), axis)
        done.append(mask)
    value_a = dp_gather(value_a, masks_a[:-1])
    out_both = dp_gather(out_both, masks_a[1:-1], masks_a[:1])
    value, value_a, x_all, out_both, prefix_gate_up, action_gate_up, action_down = tie(
        value, value_a, x_all, out_both, prefix_gate_up, action_gate_up, action_down
    )
    value_a = dp_gather(value_a, [1], masks_a[:-1]).reshape(total, -1, width_kv)
    rows_qa = action_qkv.shape[0]
    qkv_a = value_a[:, :rows_qa].reshape(-1, width_kv)
    gains = value_a[:, rows_qa].astype(F32)
    gain_ffn_p = gains[:, :rows_qp].reshape(-1)
    gain_ffn_a = gains[:, rows_qp : rows_qp + rows_qa].reshape(-1)
    qkv_p = join(value, swap(value, 1), bit_of(1), len(done)).reshape(-1, width_kv)
    out_both = dp_gather(out_both, [1], masks_a[:-1]).reshape(-1, width_p + width_a)
    out_p = out_both[:, :width_p]
    out_a = out_both[:, width_p:]
    up_far, up_near = swap(gate_up_part(1 - side), 2), widen(gate_up_part(side))
    x_all, g_rows = tie(x_all, packed(grad_out_p, grad_out_a))
    g_near = spread(g_rows)

    def slab_terms(terms_p, terms_a):
        return exchange(
            packed(
                terms_p.reshape(shard_count, slab, width_p),
                terms_a.reshape(shard_count, slab_a, width_a),
            )
        )

    def sum_slabs(terms):
        return unpacked(jnp.sum(terms.astype(F32), axis=0))

    h_attn_p = normed(x_all.reshape(whole_len, width_p).astype(F32), 1.0).astype(BF)
    h_attn_a = normed(x_a.astype(F32), 1.0).astype(BF)
    all_p = mm(h_attn_p, qkv_p).astype(BF)
    all_a = mm(h_attn_a, qkv_a).astype(BF)
    query = jnp.concatenate(
        [rows_of_heads(all_p[:, :query_here]), rows_of_heads(all_a[:, :query_here])]
    )
    kv = jnp.concatenate([all_p[:, query_here:], all_a[:, query_here:]])
    keys, vals = kv[:, :HD], kv[:, HD:]
    split = heads_here * whole_len
    is_action = jnp.arange(query.shape[0], dtype=jnp.int32) >= split
    keep = jnp.concatenate([keep_prefix, keep_action])
    keep = keep[None, :] & (
        is_action[:, None] | (jnp.arange(kv.shape[0], dtype=jnp.int32) < whole_len)[None, :]
    )
    scale = 1.0 / math.sqrt(HD)
    scores = jnp.where(keep, mm_nt(query, keys) * scale, -1e30)
    probs = jnp.exp(scores - jnp.max(scores, axis=-1, keepdims=True))
    probs = probs / jnp.sum(probs, axis=-1, keepdims=True)
    probs_low = probs.astype(BF)
    mixed = mm(probs_low, vals).astype(BF)
    mixed, up_far, up_near, g_near, down_far = tie(mixed, up_far, up_near, g_near, down_far)
    up_far = widen(up_far)
    g_far = swap(g_near, 2)
    small_far, small_near = swap(small_part(1 - side), 2), widen(small_part(side))
    mixed_p = heads_of_rows(mixed[:split], heads_here)
    mixed_a = heads_of_rows(mixed[split:], heads_here)
    mid = slab_terms(mm(mixed_p, out_p), mm(mixed_a, out_a))
    mid, small_far, small_near, down_far = tie(mid, small_far, small_near, down_far)
    small_far, down_far = widen(small_far), widen(down_far)
    mid_p, mid_a = sum_slabs(mid)
    mid_p = input_p + mid_p
    mid_a = input_a + mid_a

    h_rows = packed(normed(mid_p, gain_ffn_p), normed(mid_a, gain_ffn_a))
    near = jnp.stack([h_rows[:, cut:], swap(h_rows[:, cut:], 2)])
    first = spread(h_rows[:, :cut])
    first, near, up_far, g_far, small_far = tie(first, near, up_far, g_far, small_far)
    second = spread(near)
    first_far = swap(first, 2)
    ups = [for_cores(up_near[k], 1) + for_cores(up_far[k], 1) for k in range(outer)]
    g_p, g_a = tokens_of([g_near, g_far, swap(g_near, 1), swap(g_far, 1)], slab, width_a)
    first_core = swap(first, 1)
    second, g_p, g_a, ups, down_far, first_core, first_far = tie(
        second, g_p, g_a, ups, down_far, first_core, first_far
    )
    second_core = swap(second, 1)
    pairs = [
        (first, second[:, 0]),
        (first_far, second[:, 1]),
        (first_core, second_core[:, 0]),
        (swap(first_far, 1), second_core[:, 1]),
    ]
    h_p, h_a = tokens_of([jnp.concatenate(pair, axis=2) for pair in pairs], slab, width_a)
    downs, smalls = [], []
    for k in range(outer):
        downs += for_cores(down_near[k], 0) + for_cores(down_far[k], 0)
        smalls += for_cores(small_near[k], 1) + for_cores(small_far[k], 1)
    small = jnp.stack(smalls)
    bit = 1
    while bit < dp_count:
        pairs = small.reshape((dp_count // (2 * bit), 2, bit) + small.shape[1:])
        small = jnp.where((dp & bit) != 0, pairs[:, ::-1], pairs).reshape(small.shape)
        bit *= 2
    gate_up_a = small[:, :, : 2 * hidden_a].reshape(width_a, 2 * hidden_a)
    down_a = fold_rows(small[:, :, 2 * hidden_a :], rows_a)
    down_a = down_a.transpose(1, 0, 2).reshape(hidden_a, width_a)
    places = dp ^ jnp.arange(dp_count, dtype=jnp.int32)
    gate_up_pieces = [piece for k in range(outer) for piece in ups[k]]
    down_pieces = downs
    act_p, d_both_p, dh_p = feed_forward(h_p, g_p, places, gate_up_pieces, down_pieces)
    act_a, d_both_a, dh_a = feed_forward(h_a, g_a, places, [gate_up_a], [down_a])
    half = outer // 2

    def send_outer(terms):
        return [swap(terms[k], half * INNER) for k in sorted(terms)]

    def sum_outer(terms, got):
        terms = [terms[k] + got[k].astype(F32) for k in sorted(terms)]
        size = half
        while size > 1:
            size //= 2
            terms = [
                terms[k] + swap(terms[k + size].astype(BF), size * INNER).astype(F32)
                for k in range(size)
            ]
        return terms[0].astype(BF)

    def side_columns(values, k, far):
        width = values.shape[1] // dp_count
        place = ((dp ^ (k * INNER) ^ far) // 2) * 2 * width
        return lax.dynamic_slice_in_dim(values, place, 2 * width, 1)

    def by_core(values, far, axis):
        core = dp % 2
        size = values.shape[axis] // 2
        own = lax.dynamic_slice_in_dim(values, core * size, size, axis)
        other = lax.dynamic_slice_in_dim(values, (1 - core) * size, size, axis)
        return [swap(own, far) if far else own, swap(other, far ^ 1)]

    def gate_up_term(k, side):
        return mm_tn(side_columns(h_p, k, side), d_both_p)

    def down_term(k, side):
        return mm_tn(act_p, side_columns(g_p, k, side))

    away, here = range(half, outer), range(half)
    near, far = sum_cores(dh_p, dh_a, slab)
    terms = {k: gate_up_term(k, 2).astype(BF) for k in away}
    near, far, terms, d_both_p, act_p = tie(near, far, terms, d_both_p, act_p)
    up_far = send_outer(terms)
    second = exchange(jnp.stack([near[..., cut:], far[..., cut:]], axis=1))
    far = swap(far[..., :cut], 2)
    up_terms = {k: gate_up_term(k, 0).astype(BF) for k in away}
    down_terms = {
        side: {k: down_term(k, side).astype(BF) for k in away} for side in (2, 0)
    }
    first = (near[..., :cut].astype(F32) + far.astype(F32)).astype(BF)
    out_p_terms = down_product(act_p, places, down_pieces)
    second, first, up_terms, down_terms, out_p_terms, up_far, act_p, act_a, d_both_a = tie(
        second, first, up_terms, down_terms, out_p_terms, up_far, act_p, act_a, d_both_a
    )
    down_far, down_close = send_outer(down_terms[2]), send_outer(down_terms[0])
    first = exchange(first)
    second = jnp.sum(second.astype(F32), axis=0)
    second = second[0] + swap(second[1].astype(BF), 2).astype(F32)
    out_near, out_far = sum_cores(out_p_terms, mm(act_a, down_a).astype(BF), slab)
    (first, second, out_near, out_far, down_far, down_close, up_terms) = tie(
        first, second, out_near, out_far, down_far, down_close, up_terms
    )
    act_a, d_both_a, act_p, d_both_p, first = tie(act_a, d_both_a, act_p, d_both_p, first)
    up_close = send_outer(up_terms)
    out_far = swap(out_far, 2)
    dh = jnp.concatenate([jnp.sum(first.astype(F32), axis=0), second], axis=1)
    dh_p, dh_a = unpacked(dh)

    down_grad_a = mm_tn(act_a, g_a).reshape(hidden_a, -1, rows_a).transpose(1, 0, 2)
    small_grad = jnp.concatenate(
        [mm_tn(h_a, d_both_a).reshape(-1, rows_a, 2 * hidden_a), unfold_rows(down_grad_a)],
        axis=2,
    )
    small_terms = {
        k: lax.dynamic_slice_in_dim(small_grad, ((dp // INNER) ^ k) * INNER, INNER, 0)
        for k in range(outer)
    }
    def by_hidden(pieces, hidden):
        value = jnp.zeros((pieces[0].shape[0], INNER * hidden), F32)
        for j, piece in enumerate(pieces):
            place = (inner ^ j) * hidden
            value = lax.dynamic_update_slice_in_dim(value, piece.astype(F32), place, 1)
        return value

    def gate_up_grad(pieces, hidden):
        return jnp.stack(
            [
                by_hidden([p[:, i * hidden : (i + 1) * hidden] for p in pieces], hidden)
                for i in range(2)
            ]
        )

    def down_grad(pieces, hidden):
        value = jnp.zeros((INNER * hidden, pieces[0].shape[1]), F32)
        for j, piece in enumerate(pieces):
            place = (inner ^ j) * hidden
            value = lax.dynamic_update_slice_in_dim(value, piece.astype(F32), place, 0)
        return value

    def tall(piece):
        return jnp.concatenate(
            [piece[:, i : i + rows_a] for i in range(2 * hidden_a, piece.shape[1], rows_a)]
        )

    _, pull_ffn_p = jax.vjp(normed, mid_p, gain_ffn_p)
    from_ffn_p, gain_ffn_grad_p = pull_ffn_p(dh_p)
    d_mid_p = grad_out_p + from_ffn_p
    _, pull_ffn_a = jax.vjp(normed, mid_a, gain_ffn_a)
    from_ffn_a, gain_ffn_grad_a = pull_ffn_a(dh_a)
    d_mid_a = grad_out_a + from_ffn_a

    blocks = spread(packed(d_mid_p, d_mid_a))
    gate_up_far = sum_outer({k: gate_up_term(k, 2) for k in here}, up_far)
    down_far = sum_outer({k: down_term(k, 2) for k in here}, down_far)
    down_close = sum_outer({k: down_term(k, 0) for k in here}, down_close)
    (blocks, gate_up_far, out_far, up_close, d_both_p, gain_ffn_grad_p, gain_ffn_grad_a) = tie(
        blocks, gate_up_far, out_far, up_close, d_both_p, gain_ffn_grad_p, gain_ffn_grad_a
    )
    blocks, down_far, down_close = tie(blocks, down_far, down_close)
    down_got = by_core(down_close, 0, 1) + by_core(down_far, 2, 1)
    out_sums = (out_near.astype(F32) + out_far.astype(F32)).astype(BF)
    out_blocks = [
        lax.dynamic_index_in_dim(out_sums, (z + k) % shard_count, 0, keepdims=False)
        for k in range(shard_count)
    ]
    out_blocks = out_blocks[:1] + [shift(out_blocks[k], k) for k in range(1, shard_count)]
    far_got = by_core(gate_up_far, 2, 0)
    g_mid_p, g_mid_a = unpacked(blocks)
    g_mid_p = g_mid_p.reshape(whole_len, width_p)
    g_mid_a = g_mid_a.reshape(whole_a, width_a)
    d_mixed = jnp.concatenate(
        [
            rows_of_heads(mm_nt(g_mid_p, out_p).astype(BF)),
            rows_of_heads(mm_nt(g_mid_a, out_a).astype(BF)),
        ]
    )
    d_probs = mm_nt(d_mixed, vals)
    d_scores = (probs * (d_probs - jnp.sum(probs * d_probs, axis=-1, keepdims=True))).astype(BF)
    d_query = (mm(d_scores, keys) * scale).astype(BF)
    d_kv = jnp.concatenate(
        [(mm_tn(d_scores, query) * scale).astype(BF), mm_tn(probs_low, d_mixed).astype(BF)], axis=1
    )
    d_all_p = jnp.concatenate([heads_of_rows(d_query[:split], heads_here), d_kv[:whole_len]], axis=1)
    d_all_a = jnp.concatenate([heads_of_rows(d_query[split:], heads_here), d_kv[whole_len:]], axis=1)

    def inner_sum(value, masks):
        lead = [2] * len(masks)
        return dp_scatter(value.reshape(lead + [-1, value.shape[1]]), masks, 1).astype(BF)

    terms_p, terms_a = mm_nt(d_all_p, qkv_p), mm_nt(d_all_a, qkv_a)
    qkv_grad_p = inner_sum(mm_tn(h_attn_p, d_all_p), masks_p)
    gains_terms = jnp.concatenate(
        [gain_ffn_grad_p.reshape(total, -1), gain_ffn_grad_a.reshape(total, -1)], axis=1
    )
    gains_terms = jnp.pad(
        gains_terms[:, None], ((0, 0), (0, 7), (0, width_kv - gains_terms.shape[1]))
    )
    qkv_grad_a = mm_tn(h_attn_a, d_all_a).reshape(total, rows_qa, width_kv)
    qkv_grad_a = jnp.concatenate([qkv_grad_a, gains_terms], axis=1)
    qkv_grad_a = inner_sum(qkv_grad_a.reshape(-1, width_kv), masks_a)
    small_sent = send_outer({k: small_terms[k].astype(BF) for k in away})
    qkv_grad_p, qkv_grad_a, terms_p, terms_a, g_mid_p, d_both_p, small_sent, far_got, out_blocks = (
        tie(
            qkv_grad_p,
            qkv_grad_a,
            terms_p,
            terms_a,
            g_mid_p,
            d_both_p,
            small_sent,
            far_got,
            out_blocks,
        )
    )
    dh_terms = slab_terms(terms_p, terms_a)
    qkv_grad_p = dp_scatter(qkv_grad_p, masks_p[:-1], len(outer_masks))
    qkv_grad_a = dp_scatter(qkv_grad_a, masks_a[:-1], 1)
    out_grad = jnp.concatenate([mm_tn(mixed_p, g_mid_p), mm_tn(mixed_a, g_mid_a)], axis=1)
    out_grad = inner_sum(out_grad, masks_a)
    gate_up_close = sum_outer({k: gate_up_term(k, 0) for k in here}, up_close)
    qkv_grad_p, qkv_grad_a, gate_up_close, out_grad, down_got = tie(
        qkv_grad_p, qkv_grad_a, gate_up_close, out_grad, down_got
    )
    gate_up_got = by_core(gate_up_close, 0, 0) + far_got
    small_grad = sum_outer({k: small_terms[k] for k in here}, small_sent)
    small_got = []
    for j in range(INNER):
        piece = lax.dynamic_index_in_dim(small_grad, inner ^ j, 0, keepdims=False)
        small_got.append(swap(piece, j) if j else piece)
    qkv_grad_p = dp_scatter(qkv_grad_p, masks_p[: -1 - len(outer_masks)])
    qkv_grad_a = dp_scatter(qkv_grad_a, masks_a[:-2])
    out_grad = dp_scatter(out_grad, masks_a[:-1], 1)
    qkv_grad_p, qkv_grad_a, dh_terms, out_grad, small_got, gate_up_got = tie(
        qkv_grad_p, qkv_grad_a, dh_terms, out_grad, small_got, gate_up_got
    )
    by_slab = jnp.concatenate(
        [
            qkv_grad_p.reshape(shard_count, -1, width_kv),
            qkv_grad_a.reshape(shard_count, -1, width_kv),
        ],
        axis=1,
    )
    by_slab = exchange(by_slab.astype(BF)).astype(F32)
    ffn_p, ffn_a = unpacked(sum(block.astype(F32) for block in out_blocks))
    prefix_out = (mid_p + ffn_p).astype(BF)
    action_blocks = ring((mid_a + ffn_a).astype(BF))
    out_grad = dp_scatter(out_grad, masks_a[:-2]).astype(BF)
    out_grad = lax.ppermute(out_grad, everywhere, from_heads).astype(F32)
    dh_attn_p, dh_attn_a = sum_slabs(dh_terms)
    action_out = unring(action_blocks, 0)

    def owned(grad, weights, gains):
        query_part = [grad[k, :, :query_here] for k in range(shard_count)]
        rest = jnp.sum(grad[:, :, query_here:], axis=0)
        whole = jnp.concatenate(query_part + [rest], axis=1)
        return whole * gains, jnp.sum(whole * weights.astype(F32), axis=1)

    qkv_grad_p, gain_attn_grad_p = owned(by_slab[:, :rows_qp], prefix_qkv, own_gain_p)
    qkv_grad_a, gain_attn_grad_a = owned(
        by_slab[:, rows_qp : rows_qp + rows_qa], action_qkv, own_gain_a
    )
    gains_grad = jnp.sum(by_slab[:, rows_qp + rows_qa], axis=0)
    gains_grad_p = jnp.stack([gain_attn_grad_p, gains_grad[:rows_qp]], axis=1)
    gains_grad_a = jnp.stack(
        [gain_attn_grad_a, gains_grad[rows_qp : rows_qp + rows_qa]], axis=1
    )

    _, pull_attn_p = jax.vjp(lambda values: normed(values, 1.0), input_p)
    (from_attn_p,) = pull_attn_p(dh_attn_p)
    _, pull_attn_a = jax.vjp(lambda values: normed(values, 1.0), input_a)
    (from_attn_a,) = pull_attn_a(dh_attn_a)
    action_in_grad = unring(ring(d_mid_a + from_attn_a), 0)

    return (
        prefix_out[None],
        action_out[None, :action_rows],
        (d_mid_p + from_attn_p)[None],
        action_in_grad[None, :action_rows],
        gains_grad_p,
        gains_grad_a,
        qkv_grad_p,
        out_grad[:, :width_p],
        qkv_grad_a,
        out_grad[:, width_p:],
        gate_up_grad(gate_up_got, hidden_p),
        down_grad(down_got, hidden_p),
        gate_up_grad(small_got, hidden_a),
        down_grad([tall(piece) for piece in small_got], hidden_a),
    )


def unfold_rows(values):
    width = values.shape[-1]
    return jnp.concatenate(
        [values[:, i : i + width] for i in range(0, values.shape[1], width)], axis=2
    )


def fold_rows(values, width):
    return jnp.concatenate(
        [values[:, :, i : i + width] for i in range(0, values.shape[2], width)], axis=1
    )


def solution(mesh):
    rows = P(("dp", "mp"), None)
    tokens_p = P("dp", "mp", None)
    tokens_a = P("dp", None, None)
    gate_up = P(None, "dp", "mp")
    down = P("mp", "dp")
    per_item = P("dp")
    in_specs = (
        (tokens_p, tokens_a)
        + (per_item,) * 3
        + (rows,) * 6
        + (gate_up, down, gate_up, down)
        + (tokens_p, tokens_a)
    )
    out_specs = (
        (tokens_p, tokens_a, tokens_p, tokens_a) + (rows,) * 6 + (gate_up, down, gate_up, down)
    )
    return jax.shard_map(
        on_device, mesh=mesh, in_specs=in_specs, out_specs=out_specs, check_vma=False
    )
```
